32 devices in a mesh: ka: 2 (over x), br: 4 (over y, core), bc: 4 (over z).
Axes of the slice: x: 2, y: 2, z: 4, core: 2. Of those that a mesh axis runs over, the one named last changes fastest.
Arguments:
- green_lesser: float32 [2, 15, 2, 512, 512], P('ka', None, None, 'br', 'bc'), may hold values from -6 to 6
- screened: float32 [5, 8, 2, 512, 512], P(None, None, None, 'br', 'bc'), may hold values from -0.6 to 0.6
- slot_table: int32 [5, 2, 1], P(None, 'ka'), may hold values from 0 to 4
Outputs:
- sigma_lesser: float32 [2, 8, 2, 512, 512], P('ka', None, None, 'br', 'bc')
The draws below stay inside these ranges and needn't reach their ends.
All inputs are finite; a program needn't handle non-finite values.
Results may differ from the reference program's by a relative error of at most 0.0003.
Values sent between devices are 32-bit elements; how exact they have to be, the bound alone decides.
No kernel may reach another device: no remote copies, remote signals or barrier semaphores. Data moves between devices by JAX's collectives and lax.ppermute only.
A program may use at most 64 MiB of HBM per device.

```python
import jax
import jax.numpy as jnp
from jax import lax

NA = 512
KD = 1
NE = 8
NW = 8
NQW = 5
STOPS = 5
NK = 2
NEG = 15


def set_ends(drawn, own_key, smallest, high):
    place = [jax.random.randint(jax.random.fold_in(own_key, axis), (), 0, length) for axis, length in enumerate(drawn.shape)]
    longest = drawn.shape.index(max(drawn.shape))
    beside = place[:longest] + [(place[longest] + 1) % drawn.shape[longest]] + place[longest + 1:]
    return drawn.at[tuple(place)].set(smallest).at[tuple(beside)].set(high)


def level_of(key, dims, split, smallest, top_value):
    level = 1.0
    for axis_at, blocks in split:
        draws = jax.random.uniform(jax.random.fold_in(jax.random.fold_in(key, 6), axis_at), (blocks,), jnp.float32, smallest / len(split), top_value / len(split))
        level = level * jnp.repeat(jnp.exp(draws), dims[axis_at] // blocks).reshape((-1,) + (1,) * (len(dims) - 1 - axis_at))
    return level


def gaussian(stream_key, shape, spread, bound, shards=(), kind=jnp.bfloat16):
    gain = level_of(stream_key, shape, shards, -0.22, 0.18) if shards else 1.0
    array = jax.random.normal(stream_key, shape, jnp.float32) * spread * gain
    return jnp.minimum(jnp.maximum(array, -bound), bound).astype(kind)


def setup_inputs(seed: int = 0) -> dict:
    key_list = jax.random.split(jax.random.key(seed), 4)
    return {
        "green_lesser": gaussian(key_list[0], (NK, NEG, 2, NA, NA), 1.0, 6.0, ((0, 2), (3, 4), (4, 4)), jnp.float32),
        "screened": gaussian(key_list[1], (NQW, NW, 2, NA, NA), 0.1, 0.6, ((3, 4), (4, 4)), jnp.float32),
        "slot_table": set_ends(jax.random.randint(key_list[2], (STOPS, NK, KD), 0, NQW), jax.random.fold_in(key_list[2], 1), 0, NQW - 1).astype(jnp.int32),
    }


hop_shifts = (0, 1, -1, 2, -2)


def skew_part(values, transposed):
    return jnp.stack(((values[:, :, 0] - transposed[:, :, 0]) * 0.5, (values[:, :, 1] + transposed[:, :, 1]) * 0.5), 2)


def reference(green_lesser, screened, slot_table):
    def one_momentum(momentum):
        block_start = momentum - momentum % KD
        real_sum = jnp.zeros((NE, NA, NA), jnp.float32)
        imag_sum = jnp.zeros((NE, NA, NA), jnp.float32)
        for stop_index in range(len(hop_shifts)):
            for remote_index in range(KD):
                partner = ((block_start - KD * hop_shifts[stop_index] + remote_index) % NK).astype(jnp.int32)
                remote = lax.dynamic_index_in_dim(green_lesser, partner, 0, keepdims=False)
                slot_index = slot_table[stop_index, momentum, remote_index].astype(jnp.int32)
                chosen = lax.dynamic_index_in_dim(screened, slot_index, 0, keepdims=False)
                for freq_index in range(NW):
                    lag_start = NW - 1 - freq_index
                    window = remote[lag_start:lag_start + NE]
                    green_real = window[:, 0]
                    green_imag = window[:, 1]
                    inter_real = chosen[freq_index, 0]
                    inter_imag = chosen[freq_index, 1]
                    real_sum = real_sum - (green_real * inter_imag + green_imag * inter_real)
                    imag_sum = imag_sum + (green_real * inter_real - green_imag * inter_imag)
        return jnp.stack((real_sum, imag_sum), 1)

    unsymmetric = lax.map(one_momentum, jnp.arange(NK, dtype=jnp.int32))
    transposed = jnp.swapaxes(unsymmetric, -1, -2)
    return skew_part(unsymmetric, transposed)
```

```python
import functools

import jax
import jax.numpy as jnp
from jax import lax
from jax.experimental import pallas as pl
from jax.experimental.pallas import tpu as pltpu
from jax.sharding import PartitionSpec as P

NE = 8
HOPS = (0, 1, -1, 2, -2)
SUBLANES = 8
AXES = ("ka", "br", "bc")
VMEM_LIMIT = 32 * 1024 * 1024


def spans_of(energies, parts):
    parts = min(parts, energies)
    cuts = [energies * part // parts for part in range(parts + 1)]
    return [(low, high - low) for low, high in zip(cuts, cuts[1:])]


def correlate_kernel(first, counts, freqs, group, slots_ref, green_ref, *refs):
    del slots_ref
    screened_refs, out_refs = refs[:group], refs[group:]
    rows = green_ref.shape[3]

    def rows_step(step, carry):
        at = pl.ds(pl.multiple_of(step * SUBLANES, SUBLANES), SUBLANES)

        def inter(freq, part):
            value = screened_refs[0][0, freq, part, at, :]
            for ref in screened_refs[1:]:
                value = value + ref[0, freq, part, at, :]
            return value

        energies = sum(counts)
        real = [None] * energies
        imag = [None] * energies
        weights = [(inter(freq, 0), inter(freq, 1)) for freq in range(freqs)]
        for lag in range(energies + freqs - 1):
            green_real = green_ref[0, first + lag, 0, at, :]
            green_imag = green_ref[0, first + lag, 1, at, :]
            for energy in range(energies):
                freq = energy + freqs - 1 - lag
                if 0 <= freq < freqs:
                    inter_real, inter_imag = weights[freq]
                    real_term = green_real * inter_imag + green_imag * inter_real
                    imag_term = green_real * inter_real - green_imag * inter_imag
                    if real[energy] is None:
                        real[energy], imag[energy] = -real_term, imag_term
                    else:
                        real[energy] = real[energy] - real_term
                        imag[energy] = imag[energy] + imag_term
        energy = 0
        for out_ref, count in zip(out_refs, counts):
            for place in range(count):
                out_ref[place, 0, at, :] = real[energy]
                out_ref[place, 1, at, :] = imag[energy]
                energy += 1
        return carry

    lax.fori_loop(0, rows // SUBLANES, rows_step, 0)


def correlate(green, screened, slots, spans, row_blocks):
    freqs = screened.shape[1]
    rows, cols = green.shape[3:]
    block_rows = rows // row_blocks
    group = slots.shape[0]
    first = spans[0][0]
    counts = tuple(count for _, count in spans)

    def green_map(block, slots_ref):
        return (0, 0, 0, block, 0)

    def screened_map(place, block, slots_ref):
        return (slots_ref[place], 0, 0, block, 0)

    return pl.pallas_call(
        functools.partial(correlate_kernel, first, counts, freqs, group),
        grid_spec=pltpu.PrefetchScalarGridSpec(
            num_scalar_prefetch=1,
            grid=(row_blocks,),
            in_specs=[pl.BlockSpec((1,) + green.shape[1:3] + (block_rows, cols), green_map)]
            + [
                pl.BlockSpec((1,) + screened.shape[1:3] + (block_rows, cols), functools.partial(screened_map, place))
                for place in range(group)
            ],
            out_specs=[
                pl.BlockSpec((count, 2, block_rows, cols), lambda block, slots_ref: (0, 0, block, 0))
                for count in counts
            ],
        ),
        out_shape=[jax.ShapeDtypeStruct((count, 2, rows, cols), jnp.float32) for count in counts],
        compiler_params=pltpu.CompilerParams(vmem_limit_bytes=VMEM_LIMIT),
        name="correlate",
    )(slots, green, *([screened] * group))


def mix_kernel(received, flags_ref, own_ref, *refs):
    recv_refs = refs[:received]
    held_real_ref, held_imag_ref = refs[received : received + 2]
    raw_ref, real_ref, imag_ref = refs[received + 2 :]
    far = flags_ref[0] == 1
    count = own_ref.shape[0]
    held = held_real_ref.shape[0]
    for place in range(count):
        for part, held_ref, send_ref in ((0, held_real_ref, real_ref), (1, held_imag_ref, imag_ref)):
            value = own_ref[place, part]
            for ref in recv_refs:
                value = value + ref[place, part]
            raw_ref[place, part] = value
            if place < held:
                send_ref[place] = jnp.where(far, value, held_ref[place])
            else:
                send_ref[place] = value
    for place in range(count, held):
        for held_ref, send_ref in ((held_real_ref, real_ref), (held_imag_ref, imag_ref)):
            send_ref[place] = held_ref[place]


def mix(flags, own, received, held_real, held_imag):
    count = own.shape[0]
    tile = own.shape[2:]
    longest = max(count, held_real.shape[0])
    vmem = pl.BlockSpec(memory_space=pltpu.VMEM)
    return pl.pallas_call(
        functools.partial(mix_kernel, len(received)),
        grid_spec=pltpu.PrefetchScalarGridSpec(
            num_scalar_prefetch=1,
            grid=(),
            in_specs=[vmem] * (3 + len(received)),
            out_specs=[vmem] * 3,
        ),
        out_shape=[
            jax.ShapeDtypeStruct(own.shape, jnp.float32),
            jax.ShapeDtypeStruct((longest,) + tile, jnp.float32),
            jax.ShapeDtypeStruct((longest,) + tile, jnp.float32),
        ],
        compiler_params=pltpu.CompilerParams(vmem_limit_bytes=VMEM_LIMIT),
        name="mix",
    )(flags, own, *received, held_real, held_imag)


def skew_kernel(flags_ref, raw_ref, near_ref, far_real_ref, far_imag_ref, *refs):
    out_ref = refs[-1]

    def write(real, imag):
        out_ref[0, 0, 0] = (raw_ref[0, 0] - real.T) * 0.5
        out_ref[0, 0, 1] = (raw_ref[0, 1] + imag.T) * 0.5

    @pl.when(flags_ref[0] == 1)
    def _():
        write(far_real_ref[0], far_imag_ref[0])

    @pl.when(flags_ref[0] == 0)
    def _():
        write(near_ref[0, 0], near_ref[0, 1])

    @pl.when(flags_ref[0] == 2)
    def _():
        write(raw_ref[0, 0], raw_ref[0, 1])


def skew(flags, raw, near, far_real, far_imag, first, energies, out):
    count = raw.shape[0]
    tile = raw.shape[2:]
    pair = pl.BlockSpec((1, 2) + tile, lambda place, flags_ref: (place, 0, 0, 0))
    single = pl.BlockSpec((1,) + tile, lambda place, flags_ref: (place, 0, 0))
    operands = [raw, near, far_real, far_imag]
    in_specs = [pair, pair, single, single]
    aliases = {}
    if out is not None:
        aliases = {1 + len(operands): 0}
        operands.append(out)
        in_specs.append(pl.BlockSpec(memory_space=pl.ANY))
    return pl.pallas_call(
        skew_kernel,
        grid_spec=pltpu.PrefetchScalarGridSpec(
            num_scalar_prefetch=1,
            grid=(count,),
            in_specs=in_specs,
            out_specs=pl.BlockSpec((1, 1, 2) + tile, lambda place, flags_ref: (0, first + place, 0, 0, 0)),
        ),
        out_shape=jax.ShapeDtypeStruct((1, energies, 2) + tile, jnp.float32),
        input_output_aliases=aliases,
        compiler_params=pltpu.CompilerParams(vmem_limit_bytes=VMEM_LIMIT),
        name="skew",
    )(flags, *operands)


def grid_moves(momenta, side):
    half = side // 2

    def number(momentum, row_half, row_low, col_half, col_low):
        return (momentum * side + row_half * half + row_low) * side + col_half * half + col_low

    column_first, row_first, near = ([], []), ([], []), []
    for momentum in range(momenta):
        for a in range(2):
            for row in range(half):
                for col in range(half):
                    b = 1 - a
                    here = number(momentum, a, row, b, col)
                    mirror = number(momentum, b, col, a, row)
                    over_columns = number(momentum, a, col, a, row)
                    over_rows = number(momentum, b, row, b, col)
                    column_first[0].append((here, over_columns))
                    column_first[1].append((over_columns, mirror))
                    row_first[0].append((here, over_rows))
                    row_first[1].append((over_rows, mirror))
                    if row != col:
                        near.append((number(momentum, a, row, a, col), number(momentum, a, col, a, row)))
    return column_first, row_first, near


def on_device(parts, green_lesser, screened, slot_table):
    momenta = lax.axis_size("ka")
    side = lax.axis_size("br")
    row, col = lax.axis_index("br"), lax.axis_index("bc")
    half = side // 2
    tile = green_lesser.shape[3:]
    column_first, row_first, near_pairs = grid_moves(momenta, side)
    far = (row // half) != (col // half)
    flags = jnp.where(far, 1, jnp.where(row == col, 2, 0)).astype(jnp.int32).reshape(1)

    groups = {}
    for stop, hop in enumerate(HOPS):
        groups.setdefault(hop % momenta, []).append(stop)
    slots = {}
    for shift, stops in groups.items():
        table = slot_table
        if shift:
            table = lax.ppermute(table, "ka", [((k + shift) % momenta, k) for k in range(momenta)])
        slots[shift] = jnp.stack([table[stop, 0, 0] for stop in stops])
    spans = spans_of(NE, parts)

    own = correlate(green_lesser, screened, slots[0], spans, 4)
    arrived = [[] for _ in spans]
    for shift in groups:
        if not shift:
            continue
        pairs = [(k, (k + shift) % momenta) for k in range(momenta)]
        sent = correlate(green_lesser, screened, slots[shift], spans[:1], 4)
        sent += correlate(green_lesser, screened, slots[shift], spans[1:], 4)
        for place, part in enumerate(sent):
            arrived[place].append(lax.ppermute(part, "ka", pairs))

    raws, nears, far_parts = [], [], []
    held_real = held_imag = jnp.zeros((1,) + tile, jnp.float32)
    for place in range(len(spans)):
        raw, send_real, send_imag = mix(flags, own[place], arrived[place], held_real, held_imag)
        legs = 2 if place else 1
        held_real = lax.ppermute(send_real, AXES, sum(column_first[:legs], []))
        held_imag = lax.ppermute(send_imag, AXES, sum(row_first[:legs], []))
        nears.append(lax.ppermute(raw, AXES, near_pairs))
        raws.append(raw)
        far_parts.append((held_real, held_imag))
    held_real = lax.ppermute(held_real, AXES, column_first[1])
    held_imag = lax.ppermute(held_imag, AXES, row_first[1])
    far_parts.append((held_real, held_imag))
    out = None
    for place, (first, _) in enumerate(spans):
        out = skew(flags, raws[place], nears[place], *far_parts[place + 1], first, NE, out)
    return out


def solution(mesh):
    in_specs = (
        P("ka", None, None, "br", "bc"),
        P(None, None, None, "br", "bc"),
        P(None, "ka", None),
    )
    out_specs = P("ka", None, None, "br", "bc")
    return jax.shard_map(
        functools.partial(on_device, 4), mesh=mesh, in_specs=in_specs, out_specs=out_specs, check_vma=False
    )
```

```python
import functools

import jax
import jax.numpy as jnp
from jax import lax
from jax.experimental import pallas as pl
from jax.experimental.pallas import tpu as pltpu
from jax.sharding import PartitionSpec as P

NE = 8
TIE = True
COUNTS = (2, 2, 2, 2)
NEAR_CUTS = (1, 2, 3)
HOPS = (0, 1, -1, 2, -2)
SUBLANES = 8
AXES = ("ka", "br", "bc")
VMEM_LIMIT = 32 * 1024 * 1024


def correlate_rows(green_ref, screened_ref, table_ref, stops, first, counts, out_refs, low, high):
    freqs = screened_ref.shape[1]
    energies = sum(counts)

    def rows_step(step, carry):
        at = pl.ds(pl.multiple_of(step * SUBLANES, SUBLANES), SUBLANES)

        def inter(freq, part):
            value = screened_ref[table_ref[stops[0]], freq, part, at, :]
            for stop in stops[1:]:
                value = value + screened_ref[table_ref[stop], freq, part, at, :]
            return value

        real = [None] * energies
        imag = [None] * energies
        weights = [(inter(freq, 0), inter(freq, 1)) for freq in range(freqs)]
        for lag in range(energies + freqs - 1):
            green_real = green_ref[0, first + lag, 0, at, :]
            green_imag = green_ref[0, first + lag, 1, at, :]
            for energy in range(energies):
                freq = energy + freqs - 1 - lag
                if 0 <= freq < freqs:
                    inter_real, inter_imag = weights[freq]
                    real_term = green_real * inter_imag + green_imag * inter_real
                    imag_term = green_real * inter_real - green_imag * inter_imag
                    if real[energy] is None:
                        real[energy], imag[energy] = -real_term, imag_term
                    else:
                        real[energy] = real[energy] - real_term
                        imag[energy] = imag[energy] + imag_term
        energy = 0
        for out_ref, count in zip(out_refs, counts):
            for place in range(count):
                out_ref[place, 0, at, :] = real[energy]
                out_ref[place, 1, at, :] = imag[energy]
                energy += 1
        return carry

    lax.fori_loop(low // SUBLANES, high // SUBLANES, rows_step, 0)


def fetch_kernel(stops, first, counts, blocks, table_hbm, green_hbm, screened_hbm, green_ref, screened_ref, *refs):
    out_refs, (table_ref, table_sem, sem) = refs[:-3], refs[-3:]
    rows = green_ref.shape[3] // blocks
    table_copy = pltpu.make_async_copy(table_hbm, table_ref, table_sem)
    table_copy.start()
    copies = []
    for block in range(blocks):
        at = pl.ds(block * rows, rows)
        pair = [
            pltpu.make_async_copy(source.at[:, :, :, at], target.at[:, :, :, at], sem.at[block, which])
            for which, (source, target) in enumerate(((green_hbm, green_ref), (screened_hbm, screened_ref)))
        ]
        for copy in pair:
            copy.start()
        copies.append(pair)
    table_copy.wait()
    for block, pair in enumerate(copies):
        for copy in pair:
            copy.wait()
        correlate_rows(
            green_ref, screened_ref, table_ref, stops, first, counts, out_refs, block * rows, (block + 1) * rows
        )


def on_hbm(*arrays):
    return [pltpu.with_memory_space_constraint(array, pltpu.HBM) for array in arrays]


def run_shapes(green, spans):
    return [jax.ShapeDtypeStruct((count,) + green.shape[2:], jnp.float32) for _, count in spans]


def fetch(green, screened, table, stops, spans, blocks):
    vmem = pl.BlockSpec(memory_space=pltpu.VMEM)
    whole = pl.BlockSpec(memory_space=pltpu.HBM)
    counts = [count for _, count in spans]
    results = pl.pallas_call(
        functools.partial(fetch_kernel, stops, spans[0][0], counts, blocks),
        in_specs=[whole] * 3,
        out_specs=[vmem] * (2 + len(spans)),
        out_shape=[jax.ShapeDtypeStruct(array.shape, array.dtype) for array in (green, screened)]
        + run_shapes(green, spans),
        scratch_shapes=[
            pltpu.SMEM(table.shape, table.dtype),
            pltpu.SemaphoreType.DMA,
            pltpu.SemaphoreType.DMA((blocks, 2)),
        ],
        compiler_params=pltpu.CompilerParams(vmem_limit_bytes=VMEM_LIMIT),
        name="fetch",
    )(table, green, screened)
    return results[0], results[1], results[2:]


def correlate_kernel(stops, first, counts, table_ref, green_ref, screened_ref, *out_refs):
    correlate_rows(
        green_ref, screened_ref, table_ref, stops, first, counts, out_refs, 0, green_ref.shape[3]
    )


def correlate(green, screened, table, stops, spans):
    if not spans:
        return []
    vmem = pl.BlockSpec(memory_space=pltpu.VMEM)
    counts = [count for _, count in spans]
    return pl.pallas_call(
        functools.partial(correlate_kernel, stops, spans[0][0], counts),
        in_specs=[pl.BlockSpec(memory_space=pltpu.SMEM), vmem, vmem],
        out_specs=[vmem] * len(spans),
        out_shape=run_shapes(green, spans),
        compiler_params=pltpu.CompilerParams(vmem_limit_bytes=VMEM_LIMIT),
        name="correlate",
    )(table, green, screened)


def place_of_device():
    row, col = lax.axis_index("br"), lax.axis_index("bc")
    half = lax.axis_size("br") // 2
    return (row // half) != (col // half), row == col


def mix_kernel(received, held, own_ref, *refs):
    recv_refs = refs[:received]
    held_refs = refs[received : received + sum(held)]
    raw_ref, col_ref, row_ref = refs[received + sum(held) :]
    far, _ = place_of_device()
    queue = list(held_refs)
    holds = [queue.pop(0) if has else None for has in held]
    count = own_ref.shape[0]
    for part, hold_ref, send_ref in zip((0, 1), holds, (col_ref, row_ref)):
        for place in range(send_ref.shape[0]):
            value = None
            if place < count:
                value = own_ref[place, part]
                for ref in recv_refs:
                    value = value + ref[place, part]
                raw_ref[place, part] = value
            if hold_ref is not None and place < hold_ref.shape[0]:
                kept = hold_ref[place]
                value = kept if value is None else jnp.where(far, value, kept)
            if value is not None:
                send_ref[place] = value


def mix(own, received, held_columns, held_rows):
    vmem = pl.BlockSpec(memory_space=pltpu.VMEM)
    held = [array is not None for array in (held_columns, held_rows)]
    holds = [array for array in (held_columns, held_rows) if array is not None]
    lengths = [max(own.shape[0], array.shape[0] if array is not None else 0) for array in (held_columns, held_rows)]
    shapes = [own.shape] + [(length,) + own.shape[2:] for length in lengths]
    return pl.pallas_call(
        functools.partial(mix_kernel, len(received), held),
        in_specs=[vmem] * (1 + len(received) + len(holds)),
        out_specs=[vmem] * 3,
        out_shape=[jax.ShapeDtypeStruct(shape, jnp.float32) for shape in shapes],
        compiler_params=pltpu.CompilerParams(vmem_limit_bytes=VMEM_LIMIT),
        name="mix",
    )(own, *received, *holds)


def pack_kernel(*refs):
    out_ref = refs[-1]
    far, _ = place_of_device()

    @pl.when(jnp.logical_not(far))
    def _():
        at = 0
        for ref in refs[:-1]:
            out_ref[pl.ds(at, ref.shape[0])] = ref[...]
            at += ref.shape[0]


def pack(raws):
    if len(raws) == 1:
        return raws[0]
    vmem = pl.BlockSpec(memory_space=pltpu.VMEM)
    return pl.pallas_call(
        pack_kernel,
        in_specs=[vmem] * len(raws),
        out_specs=vmem,
        out_shape=jax.ShapeDtypeStruct((sum(raw.shape[0] for raw in raws),) + raws[0].shape[1:], jnp.float32),
        compiler_params=pltpu.CompilerParams(vmem_limit_bytes=VMEM_LIMIT),
        name="pack",
    )(*raws)


def skew_kernel(which, places, *refs):
    width = 2 + len(which)
    parts = [refs[width * at : width * (at + 1)] for at in range(len(places))]
    out_ref, done_ref, sem = refs[-3:]
    far, own = place_of_device()
    start = places[0][0]

    def write(partner):
        for (raw_ref, near_ref, *far_refs), (first, near_first, far_firsts) in zip(parts, places):
            for at in range(raw_ref.shape[0]):
                for slot, (kind, far_ref, far_first) in enumerate(zip(which, far_refs, far_firsts)):
                    raw = raw_ref[at, kind]
                    mirror = partner(raw, near_ref, near_first + at, kind, far_ref, far_first + at).T
                    done_ref[first - start + at, slot] = (raw + mirror if kind else raw - mirror) * 0.5

    @pl.when(far)
    def _():
        write(lambda raw, near_ref, near_at, kind, far_ref, far_at: far_ref[far_at])

    @pl.when(jnp.logical_and(jnp.logical_not(far), jnp.logical_not(own)))
    def _():
        write(lambda raw, near_ref, near_at, kind, far_ref, far_at: near_ref[near_at, kind])

    @pl.when(own)
    def _():
        write(lambda raw, near_ref, near_at, kind, far_ref, far_at: raw)

    target = out_ref.at[0, pl.ds(start, done_ref.shape[0]), pl.ds(which[0], len(which))]
    copy = pltpu.make_async_copy(done_ref, target, sem)
    copy.start()
    copy.wait()


def skew(parts, which, energies, out):
    vmem = pl.BlockSpec(memory_space=pltpu.VMEM)
    whole = pl.BlockSpec(memory_space=pl.ANY)
    operands = [array for _, raw, near, _, fars, _ in parts for array in (raw, near, *fars)]
    in_specs = [vmem] * len(operands)
    aliases = {}
    if out is not None:
        aliases = {len(operands): 0}
        operands.append(out)
        in_specs.append(whole)
    shape = parts[0][1].shape
    count = sum(raw.shape[0] for _, raw, *_ in parts)
    return pl.pallas_call(
        functools.partial(skew_kernel, which, [(part[0], part[3], part[5]) for part in parts]),
        in_specs=in_specs,
        out_specs=whole,
        out_shape=jax.ShapeDtypeStruct((1, energies) + shape[1:], jnp.float32),
        scratch_shapes=[pltpu.VMEM((count, len(which)) + shape[2:], jnp.float32), pltpu.SemaphoreType.DMA],
        input_output_aliases=aliases,
        compiler_params=pltpu.CompilerParams(vmem_limit_bytes=VMEM_LIMIT),
        name="skew",
    )(*operands)


def grid_moves(momenta, side):
    half = side // 2

    def number(momentum, row_half, row_low, col_half, col_low):
        return (momentum * side + row_half * half + row_low) * side + col_half * half + col_low

    over_columns, over_rows, near = ([], []), ([], []), []
    for momentum in range(momenta):
        for a in range(2):
            for row in range(half):
                for col in range(half):
                    b = 1 - a
                    here = number(momentum, a, row, b, col)
                    mirror = number(momentum, b, col, a, row)
                    by_columns = number(momentum, a, col, a, row)
                    by_rows = number(momentum, b, row, b, col)
                    over_columns[0].append((here, by_columns))
                    over_columns[1].append((by_rows, mirror))
                    over_rows[0].append((here, by_rows))
                    over_rows[1].append((by_columns, mirror))
                    if row != col:
                        near.append((number(momentum, a, row, a, col), number(momentum, a, col, a, row)))
    return over_columns, over_rows, near


def send(array, axes, pairs, what):
    with jax.named_scope(what):
        return lax.ppermute(array, axes, pairs)


def on_device(counts, near_cuts, green_lesser, screened, slot_table):
    momenta = lax.axis_size("ka")
    over_columns, over_rows, near_pairs = grid_moves(momenta, lax.axis_size("br"))
    groups = {}
    for stop, hop in enumerate(HOPS):
        groups.setdefault(hop % momenta, []).append(stop)
    spans = [(sum(counts[:run]), count) for run, count in enumerate(counts)]
    runs = len(spans)
    groups_near = list(zip((0, *near_cuts), (*near_cuts, runs)))

    tables = {}
    for shift in groups:
        table = slot_table
        if shift:
            table = lax.ppermute(table, "ka", [((k + shift) % momenta, k) for k in range(momenta)])
        tables[shift] = table.reshape(len(HOPS))
    green, inter, own = fetch(*on_hbm(green_lesser, screened, tables.pop(0)), groups.pop(0), spans, 4)

    terms = [{} for _ in spans]
    for some in (range(1), range(1, runs)):
        for shift, stops in groups.items():
            found = correlate(green, inter, tables[shift], stops, [spans[run] for run in some])
            for run, term in zip(some, found):
                terms[run][shift] = term

    def exchange(run):
        return [
            send(term, "ka", [(k, (k + shift) % momenta) for k in range(momenta)], f"momentum_{run}")
            for shift, term in terms[run].items()
        ]

    arrived = [exchange(run) for run in range(runs)]
    raws, by_columns, by_rows = [], [], []
    for run in range(runs):
        raw, over_first, over_second = mix(
            own[run],
            arrived[run],
            by_rows[run - 1] if run >= 1 else None,
            by_columns[run - 2] if run >= 2 else None,
        )
        raws.append(raw)
        by_columns.append(send(over_first, AXES, sum(over_columns, []), f"columns_{run}"))
        by_rows.append(send(over_second, AXES, sum(over_rows, []), f"rows_{run}"))
    nears, near_places = [], []
    for low, high in groups_near:
        near = send(pack(raws[low:high]), AXES, near_pairs, f"near_{low}")
        for run in range(low, high):
            nears.append(near)
            near_places.append(spans[run][0] - spans[low][0])
    by_columns.append(send(by_rows[-1], AXES, over_columns[1], f"columns_{runs}"))

    def part(run, fars, far_firsts):
        return spans[run][0], raws[run], nears[run], near_places[run], fars, far_firsts

    out = None
    for run in range(runs - 2):
        out = skew([part(run, [by_rows[run + 2], by_columns[run + 1]], [0, 0])], (0, 1), NE, out)
    last = by_columns[runs - 1]
    if out is not None and TIE:
        last, out = lax.optimization_barrier((last, out))
    by_rows.append(send(by_columns[runs - 2], AXES, over_rows[1], f"rows_{runs}"))
    by_rows.append(send(last, AXES, over_rows[1], f"rows_{runs + 1}"))
    ends = (runs - 2, runs - 1)
    out = skew([part(run, [by_columns[run + 1]], [0]) for run in ends], (1,), NE, out)
    return skew([part(run, [by_rows[run + 2]], [0]) for run in ends], (0,), NE, out)


def solution(mesh):
    in_specs = (
        P("ka", None, None, "br", "bc"),
        P(None, None, None, "br", "bc"),
        P(None, "ka", None),
    )
    out_specs = P("ka", None, None, "br", "bc")
    return jax.shard_map(
        functools.partial(on_device, COUNTS, NEAR_CUTS), mesh=mesh, in_specs=in_specs, out_specs=out_specs, check_vma=False
    )
```

```python
import functools

import jax
import jax.numpy as jnp
from jax import lax
from jax.experimental import pallas as pl
from jax.experimental.pallas import tpu as pltpu
from jax.sharding import PartitionSpec as P

NE = 8
TIE = True
BLOCKS = 2
OWN_TIE = True
FLOPS = 20_000_000_000
COUNTS = (2,2,2,2)
NEAR_CUTS = (1,3)
HOPS = (0, 1, -1, 2, -2)
SUBLANES = 8
AXES = ("ka", "br", "bc")
VMEM_LIMIT = 32 * 1024 * 1024


def correlate_rows(green_ref, screened_ref, table_ref, stops, first, counts, out_refs, low, high):
    freqs = screened_ref.shape[1]
    energies = sum(counts)

    def rows_step(step, carry):
        at = pl.ds(pl.multiple_of(step * SUBLANES, SUBLANES), SUBLANES)

        def inter(freq, part):
            value = screened_ref[table_ref[stops[0]], freq, part, at, :]
            for stop in stops[1:]:
                value = value + screened_ref[table_ref[stop], freq, part, at, :]
            return value

        real = [None] * energies
        imag = [None] * energies
        weights = [(inter(freq, 0), inter(freq, 1)) for freq in range(freqs)]
        for lag in range(energies + freqs - 1):
            green_real = green_ref[0, first + lag, 0, at, :]
            green_imag = green_ref[0, first + lag, 1, at, :]
            for energy in range(energies):
                freq = energy + freqs - 1 - lag
                if 0 <= freq < freqs:
                    inter_real, inter_imag = weights[freq]
                    real_term = green_real * inter_imag + green_imag * inter_real
                    imag_term = green_real * inter_real - green_imag * inter_imag
                    if real[energy] is None:
                        real[energy], imag[energy] = -real_term, imag_term
                    else:
                        real[energy] = real[energy] - real_term
                        imag[energy] = imag[energy] + imag_term
        energy = 0
        for out_ref, count in zip(out_refs, counts):
            for place in range(count):
                out_ref[place, 0, at, :] = real[energy]
                out_ref[place, 1, at, :] = imag[energy]
                energy += 1
        return carry

    lax.fori_loop(low // SUBLANES, high // SUBLANES, rows_step, 0)


def fetch_kernel(blocks, green_hbm, screened_hbm, green_ref, screened_ref, sem):
    copies = []
    for which, (source, target) in enumerate(((screened_hbm, screened_ref), (green_hbm, green_ref))):
        rows = source.shape[3] // blocks
        for block in range(blocks):
            at = pl.ds(block * rows, rows)
            copies.append(
                pltpu.make_async_copy(source.at[:, :, :, at], target.at[:, :, :, at], sem.at[which, block])
            )
    for copy in copies:
        copy.start()
    for copy in copies:
        copy.wait()


def on_hbm(*arrays):
    return [pltpu.with_memory_space_constraint(array, pltpu.HBM) for array in arrays]


def fetch(green, screened, blocks):
    vmem = pl.BlockSpec(memory_space=pltpu.VMEM)
    return pl.pallas_call(
        functools.partial(fetch_kernel, blocks),
        in_specs=[pl.BlockSpec(memory_space=pltpu.HBM)] * 2,
        out_specs=[vmem] * 2,
        out_shape=[jax.ShapeDtypeStruct(array.shape, array.dtype) for array in (green, screened)],
        scratch_shapes=[pltpu.SemaphoreType.DMA((2, blocks))],
        compiler_params=pltpu.CompilerParams(vmem_limit_bytes=VMEM_LIMIT),
        name="fetch",
    )(*on_hbm(green, screened))


def run_shapes(green, spans):
    return [jax.ShapeDtypeStruct((count,) + green.shape[2:], jnp.float32) for _, count in spans]


def correlate_kernel(stops, first, counts, table_ref, green_ref, screened_ref, *out_refs):
    correlate_rows(
        green_ref, screened_ref, table_ref, stops, first, counts, out_refs, 0, green_ref.shape[3]
    )


def correlate(green, screened, table, stops, spans):
    if not spans:
        return []
    vmem = pl.BlockSpec(memory_space=pltpu.VMEM)
    counts = [count for _, count in spans]
    return pl.pallas_call(
        functools.partial(correlate_kernel, stops, spans[0][0], counts),
        in_specs=[pl.BlockSpec(memory_space=pltpu.SMEM), vmem, vmem],
        out_specs=[vmem] * len(spans),
        out_shape=run_shapes(green, spans),
        compiler_params=pltpu.CompilerParams(vmem_limit_bytes=VMEM_LIMIT),
        name="correlate",
    )(table, green, screened)


def place_of_device():
    row, col = lax.axis_index("br"), lax.axis_index("bc")
    half = lax.axis_size("br") // 2
    return (row // half) != (col // half), row == col


def mix_kernel(received, held, own_ref, *refs):
    recv_refs = refs[:received]
    held_refs = refs[received : received + sum(held)]
    raw_ref, col_ref, row_ref = refs[received + sum(held) :]
    far, _ = place_of_device()
    queue = list(held_refs)
    holds = [queue.pop(0) if has else None for has in held]
    count = own_ref.shape[0]
    for part, hold_ref, send_ref in zip((0, 1), holds, (col_ref, row_ref)):
        for place in range(send_ref.shape[0]):
            value = None
            if place < count:
                value = own_ref[place, part]
                for ref in recv_refs:
                    value = value + ref[place, part]
                raw_ref[place, part] = value
            if hold_ref is not None and place < hold_ref.shape[0]:
                kept = hold_ref[place]
                value = kept if value is None else jnp.where(far, value, kept)
            if value is not None:
                send_ref[place] = value


def mix(own, received, held_columns, held_rows):
    vmem = pl.BlockSpec(memory_space=pltpu.VMEM)
    held = [array is not None for array in (held_columns, held_rows)]
    holds = [array for array in (held_columns, held_rows) if array is not None]
    lengths = [max(own.shape[0], array.shape[0] if array is not None else 0) for array in (held_columns, held_rows)]
    shapes = [own.shape] + [(length,) + own.shape[2:] for length in lengths]
    return pl.pallas_call(
        functools.partial(mix_kernel, len(received), held),
        in_specs=[vmem] * (1 + len(received) + len(holds)),
        out_specs=[vmem] * 3,
        out_shape=[jax.ShapeDtypeStruct(shape, jnp.float32) for shape in shapes],
        compiler_params=pltpu.CompilerParams(vmem_limit_bytes=VMEM_LIMIT),
        name="mix", cost_estimate=pl.CostEstimate(flops=FLOPS, bytes_accessed=1000000, transcendentals=0),
    )(own, *received, *holds)


def pack_kernel(*refs):
    out_ref = refs[-1]
    far, _ = place_of_device()

    @pl.when(jnp.logical_not(far))
    def _():
        at = 0
        for ref in refs[:-1]:
            out_ref[pl.ds(at, ref.shape[0])] = ref[...]
            at += ref.shape[0]


def pack(raws):
    if len(raws) == 1:
        return raws[0]
    vmem = pl.BlockSpec(memory_space=pltpu.VMEM)
    return pl.pallas_call(
        pack_kernel,
        in_specs=[vmem] * len(raws),
        out_specs=vmem,
        out_shape=jax.ShapeDtypeStruct((sum(raw.shape[0] for raw in raws),) + raws[0].shape[1:], jnp.float32),
        compiler_params=pltpu.CompilerParams(vmem_limit_bytes=VMEM_LIMIT),
        name="pack",
    )(*raws)


def skew_kernel(which, places, *refs):
    width = 2 + len(which)
    parts = [refs[width * at : width * (at + 1)] for at in range(len(places))]
    out_ref, done_ref, sem = refs[-3:]
    far, own = place_of_device()
    start = places[0][0]

    def write(partner):
        for (raw_ref, near_ref, *far_refs), (first, near_first, far_firsts) in zip(parts, places):
            for at in range(raw_ref.shape[0]):
                for slot, (kind, far_ref, far_first) in enumerate(zip(which, far_refs, far_firsts)):
                    raw = raw_ref[at, kind]
                    mirror = partner(raw, near_ref, near_first + at, kind, far_ref, far_first + at).T
                    done_ref[first - start + at, slot] = (raw + mirror if kind else raw - mirror) * 0.5

    @pl.when(far)
    def _():
        write(lambda raw, near_ref, near_at, kind, far_ref, far_at: far_ref[far_at])

    @pl.when(jnp.logical_and(jnp.logical_not(far), jnp.logical_not(own)))
    def _():
        write(lambda raw, near_ref, near_at, kind, far_ref, far_at: near_ref[near_at, kind])

    @pl.when(own)
    def _():
        write(lambda raw, near_ref, near_at, kind, far_ref, far_at: raw)

    target = out_ref.at[0, pl.ds(start, done_ref.shape[0]), pl.ds(which[0], len(which))]
    copy = pltpu.make_async_copy(done_ref, target, sem)
    copy.start()
    copy.wait()


def skew(parts, which, energies, out):
    vmem = pl.BlockSpec(memory_space=pltpu.VMEM)
    whole = pl.BlockSpec(memory_space=pl.ANY)
    operands = [array for _, raw, near, _, fars, _ in parts for array in (raw, near, *fars)]
    in_specs = [vmem] * len(operands)
    aliases = {}
    if out is not None:
        aliases = {len(operands): 0}
        operands.append(out)
        in_specs.append(whole)
    shape = parts[0][1].shape
    count = sum(raw.shape[0] for _, raw, *_ in parts)
    return pl.pallas_call(
        functools.partial(skew_kernel, which, [(part[0], part[3], part[5]) for part in parts]),
        in_specs=in_specs,
        out_specs=whole,
        out_shape=jax.ShapeDtypeStruct((1, energies) + shape[1:], jnp.float32),
        scratch_shapes=[pltpu.VMEM((count, len(which)) + shape[2:], jnp.float32), pltpu.SemaphoreType.DMA],
        input_output_aliases=aliases,
        compiler_params=pltpu.CompilerParams(vmem_limit_bytes=VMEM_LIMIT),
        name="skew",
    )(*operands)


def grid_moves(momenta, side):
    half = side // 2

    def number(momentum, row_half, row_low, col_half, col_low):
        return (momentum * side + row_half * half + row_low) * side + col_half * half + col_low

    over_columns, over_rows, near = ([], []), ([], []), []
    for momentum in range(momenta):
        for a in range(2):
            for row in range(half):
                for col in range(half):
                    b = 1 - a
                    here = number(momentum, a, row, b, col)
                    mirror = number(momentum, b, col, a, row)
                    by_columns = number(momentum, a, col, a, row)
                    by_rows = number(momentum, b, row, b, col)
                    over_columns[0].append((here, by_columns))
                    over_columns[1].append((by_rows, mirror))
                    over_rows[0].append((here, by_rows))
                    over_rows[1].append((by_columns, mirror))
                    if row != col:
                        near.append((number(momentum, a, row, a, col), number(momentum, a, col, a, row)))
    return over_columns, over_rows, near


def send(array, axes, pairs, what):
    with jax.named_scope(what):
        return lax.ppermute(array, axes, pairs)


def on_device(counts, near_cuts, green_lesser, screened, slot_table):
    momenta = lax.axis_size("ka")
    over_columns, over_rows, near_pairs = grid_moves(momenta, lax.axis_size("br"))
    groups = {}
    for stop, hop in enumerate(HOPS):
        groups.setdefault(hop % momenta, []).append(stop)
    spans = [(sum(counts[:run]), count) for run, count in enumerate(counts)]
    runs = len(spans)
    groups_near = list(zip((0, *near_cuts), (*near_cuts, runs)))

    tables = {}
    for shift in groups:
        table = slot_table
        if shift:
            table = lax.ppermute(table, "ka", [((k + shift) % momenta, k) for k in range(momenta)])
        tables[shift] = table.reshape(len(HOPS))
    green, inter = fetch(green_lesser, screened, BLOCKS)
    own_table, own_stops = tables.pop(0), groups.pop(0)

    terms = [{} for _ in spans]
    for some in (range(1), range(1, runs)):
        for shift, stops in groups.items():
            found = correlate(green, inter, tables[shift], stops, [spans[run] for run in some])
            for run, term in zip(some, found):
                terms[run][shift] = term

    def exchange(run):
        return [
            send(term, "ka", [(k, (k + shift) % momenta) for k in range(momenta)], f"momentum_{run}")
            for shift, term in terms[run].items()
        ]

    if runs > 1 and OWN_TIE:
        own_table, terms[0] = lax.optimization_barrier((own_table, terms[0]))
    own = correlate(green, inter, own_table, own_stops, spans)
    arrived = [exchange(run) for run in range(runs)]
    raws, by_columns, by_rows = [], [], []
    for run in range(runs):
        raw, over_first, over_second = mix(
            own[run],
            arrived[run],
            by_rows[run - 1] if run >= 1 else None,
            by_columns[run - 2] if run >= 2 else None,
        )
        raws.append(raw)
        by_columns.append(send(over_first, AXES, sum(over_columns, []), f"columns_{run}"))
        by_rows.append(send(over_second, AXES, sum(over_rows, []), f"rows_{run}"))
    nears, near_places = [], []
    for low, high in groups_near:
        near = send(pack(raws[low:high]), AXES, near_pairs, f"near_{low}")
        for run in range(low, high):
            nears.append(near)
            near_places.append(spans[run][0] - spans[low][0])
    by_columns.append(send(by_rows[-1], AXES, over_columns[1], f"columns_{runs}"))

    def part(run, fars, far_firsts):
        return spans[run][0], raws[run], nears[run], near_places[run], fars, far_firsts

    out = None
    for run in range(runs - 2):
        out = skew([part(run, [by_rows[run + 2], by_columns[run + 1]], [0, 0])], (0, 1), NE, out)
    last = by_columns[runs - 1]
    if out is not None and TIE:
        last, out = lax.optimization_barrier((last, out))
    by_rows.append(send(by_columns[runs - 2], AXES, over_rows[1], f"rows_{runs}"))
    by_rows.append(send(last, AXES, over_rows[1], f"rows_{runs + 1}"))
    ends = (runs - 2, runs - 1)
    out = skew([part(run, [by_columns[run + 1]], [0]) for run in ends], (1,), NE, out)
    return skew([part(run, [by_rows[run + 2]], [0]) for run in ends], (0,), NE, out)


def solution(mesh):
    in_specs = (
        P("ka", None, None, "br", "bc"),
        P(None, None, None, "br", "bc"),
        P(None, "ka", None),
    )
    out_specs = P("ka", None, None, "br", "bc")
    return jax.shard_map(
        functools.partial(on_device, COUNTS, NEAR_CUTS), mesh=mesh, in_specs=in_specs, out_specs=out_specs, check_vma=False
    )
```

```python
import functools

import jax
import jax.numpy as jnp
from jax import lax
from jax.experimental import pallas as pl
from jax.experimental.pallas import tpu as pltpu
from jax.sharding import PartitionSpec as P

NE = 8
TIE = True
BLOCKS = 2
NEAR_LAST = False
ROWS_LAST = False
SKEW_TIE = True
OWN_TIE = True
FLOPS = 20_000_000_000
COUNTS = (2,2,2,2)
NEAR_CUTS = (3,)
HOPS = (0, 1, -1, 2, -2)
SUBLANES = 8
AXES = ("ka", "br", "bc")
VMEM_LIMIT = 32 * 1024 * 1024


def correlate_rows(green_ref, screened_ref, table_ref, stops, first, counts, out_refs, low, high):
    freqs = screened_ref.shape[1]
    energies = sum(counts)

    def rows_step(step, carry):
        at = pl.ds(pl.multiple_of(step * SUBLANES, SUBLANES), SUBLANES)

        def inter(freq, part):
            value = screened_ref[table_ref[stops[0]], freq, part, at, :]
            for stop in stops[1:]:
                value = value + screened_ref[table_ref[stop], freq, part, at, :]
            return value

        real = [None] * energies
        imag = [None] * energies
        weights = [(inter(freq, 0), inter(freq, 1)) for freq in range(freqs)]
        for lag in range(energies + freqs - 1):
            green_real = green_ref[0, first + lag, 0, at, :]
            green_imag = green_ref[0, first + lag, 1, at, :]
            for energy in range(energies):
                freq = energy + freqs - 1 - lag
                if 0 <= freq < freqs:
                    inter_real, inter_imag = weights[freq]
                    real_term = green_real * inter_imag + green_imag * inter_real
                    imag_term = green_real * inter_real - green_imag * inter_imag
                    if real[energy] is None:
                        real[energy], imag[energy] = -real_term, imag_term
                    else:
                        real[energy] = real[energy] - real_term
                        imag[energy] = imag[energy] + imag_term
        energy = 0
        for out_ref, count in zip(out_refs, counts):
            for place in range(count):
                out_ref[place, 0, at, :] = real[energy]
                out_ref[place, 1, at, :] = imag[energy]
                energy += 1
        return carry

    lax.fori_loop(low // SUBLANES, high // SUBLANES, rows_step, 0)


def fetch_kernel(blocks, green_hbm, screened_hbm, green_ref, screened_ref, sem):
    copies = []
    for which, (source, target) in enumerate(((screened_hbm, screened_ref), (green_hbm, green_ref))):
        rows = source.shape[3] // blocks
        for block in range(blocks):
            at = pl.ds(block * rows, rows)
            copies.append(
                pltpu.make_async_copy(source.at[:, :, :, at], target.at[:, :, :, at], sem.at[which, block])
            )
    for copy in copies:
        copy.start()
    for copy in copies:
        copy.wait()


def on_hbm(*arrays):
    return [pltpu.with_memory_space_constraint(array, pltpu.HBM) for array in arrays]


def fetch(green, screened, blocks):
    vmem = pl.BlockSpec(memory_space=pltpu.VMEM)
    return pl.pallas_call(
        functools.partial(fetch_kernel, blocks),
        in_specs=[pl.BlockSpec(memory_space=pltpu.HBM)] * 2,
        out_specs=[vmem] * 2,
        out_shape=[jax.ShapeDtypeStruct(array.shape, array.dtype) for array in (green, screened)],
        scratch_shapes=[pltpu.SemaphoreType.DMA((2, blocks))],
        compiler_params=pltpu.CompilerParams(vmem_limit_bytes=VMEM_LIMIT),
        name="fetch",
    )(*on_hbm(green, screened))


def run_shapes(green, spans):
    return [jax.ShapeDtypeStruct((count,) + green.shape[2:], jnp.float32) for _, count in spans]


def correlate_kernel(stops, first, counts, table_ref, green_ref, screened_ref, *out_refs):
    correlate_rows(
        green_ref, screened_ref, table_ref, stops, first, counts, out_refs, 0, green_ref.shape[3]
    )


def correlate(green, screened, table, stops, spans):
    if not spans:
        return []
    vmem = pl.BlockSpec(memory_space=pltpu.VMEM)
    counts = [count for _, count in spans]
    return pl.pallas_call(
        functools.partial(correlate_kernel, stops, spans[0][0], counts),
        in_specs=[pl.BlockSpec(memory_space=pltpu.SMEM), vmem, vmem],
        out_specs=[vmem] * len(spans),
        out_shape=run_shapes(green, spans),
        compiler_params=pltpu.CompilerParams(vmem_limit_bytes=VMEM_LIMIT),
        name="correlate",
    )(table, green, screened)


def place_of_device():
    row, col = lax.axis_index("br"), lax.axis_index("bc")
    half = lax.axis_size("br") // 2
    return (row // half) != (col // half), row == col


def mix_kernel(received, held, own_ref, *refs):
    recv_refs = refs[:received]
    held_refs = refs[received : received + sum(held)]
    raw_ref, col_ref, row_ref = refs[received + sum(held) :]
    far, _ = place_of_device()
    queue = list(held_refs)
    holds = [queue.pop(0) if has else None for has in held]
    count = own_ref.shape[0]
    for part, hold_ref, send_ref in zip((0, 1), holds, (col_ref, row_ref)):
        for place in range(send_ref.shape[0]):
            value = None
            if place < count:
                value = own_ref[place, part]
                for ref in recv_refs:
                    value = value + ref[place, part]
                raw_ref[place, part] = value
            if hold_ref is not None and place < hold_ref.shape[0]:
                kept = hold_ref[place]
                value = kept if value is None else jnp.where(far, value, kept)
            if value is not None:
                send_ref[place] = value


def mix(own, received, held_columns, held_rows):
    vmem = pl.BlockSpec(memory_space=pltpu.VMEM)
    held = [array is not None for array in (held_columns, held_rows)]
    holds = [array for array in (held_columns, held_rows) if array is not None]
    lengths = [max(own.shape[0], array.shape[0] if array is not None else 0) for array in (held_columns, held_rows)]
    shapes = [own.shape] + [(length,) + own.shape[2:] for length in lengths]
    return pl.pallas_call(
        functools.partial(mix_kernel, len(received), held),
        in_specs=[vmem] * (1 + len(received) + len(holds)),
        out_specs=[vmem] * 3,
        out_shape=[jax.ShapeDtypeStruct(shape, jnp.float32) for shape in shapes],
        compiler_params=pltpu.CompilerParams(vmem_limit_bytes=VMEM_LIMIT),
        name="mix", cost_estimate=pl.CostEstimate(flops=FLOPS, bytes_accessed=1000000, transcendentals=0),
    )(own, *received, *holds)


def pack_kernel(*refs):
    out_ref = refs[-1]
    far, _ = place_of_device()

    @pl.when(jnp.logical_not(far))
    def _():
        at = 0
        for ref in refs[:-1]:
            out_ref[pl.ds(at, ref.shape[0])] = ref[...]
            at += ref.shape[0]


def pack(raws):
    if len(raws) == 1:
        return raws[0]
    vmem = pl.BlockSpec(memory_space=pltpu.VMEM)
    return pl.pallas_call(
        pack_kernel,
        in_specs=[vmem] * len(raws),
        out_specs=vmem,
        out_shape=jax.ShapeDtypeStruct((sum(raw.shape[0] for raw in raws),) + raws[0].shape[1:], jnp.float32),
        compiler_params=pltpu.CompilerParams(vmem_limit_bytes=VMEM_LIMIT),
        name="pack",
    )(*raws)


def skew_kernel(which, places, *refs):
    width = 2 + len(which)
    parts = [refs[width * at : width * (at + 1)] for at in range(len(places))]
    out_ref, done_ref, sem = refs[-3:]
    far, own = place_of_device()
    start = places[0][0]

    def write(partner):
        for (raw_ref, near_ref, *far_refs), (first, near_first, far_firsts) in zip(parts, places):
            for at in range(raw_ref.shape[0]):
                for slot, (kind, far_ref, far_first) in enumerate(zip(which, far_refs, far_firsts)):
                    raw = raw_ref[at, kind]
                    mirror = partner(raw, near_ref, near_first + at, kind, far_ref, far_first + at).T
                    done_ref[first - start + at, slot] = (raw + mirror if kind else raw - mirror) * 0.5

    @pl.when(far)
    def _():
        write(lambda raw, near_ref, near_at, kind, far_ref, far_at: far_ref[far_at])

    @pl.when(jnp.logical_and(jnp.logical_not(far), jnp.logical_not(own)))
    def _():
        write(lambda raw, near_ref, near_at, kind, far_ref, far_at: near_ref[near_at, kind])

    @pl.when(own)
    def _():
        write(lambda raw, near_ref, near_at, kind, far_ref, far_at: raw)

    target = out_ref.at[0, pl.ds(start, done_ref.shape[0]), pl.ds(which[0], len(which))]
    copy = pltpu.make_async_copy(done_ref, target, sem)
    copy.start()
    copy.wait()


def skew(parts, which, energies, out):
    vmem = pl.BlockSpec(memory_space=pltpu.VMEM)
    whole = pl.BlockSpec(memory_space=pl.ANY)
    operands = [array for _, raw, near, _, fars, _ in parts for array in (raw, near, *fars)]
    in_specs = [vmem] * len(operands)
    aliases = {}
    if out is not None:
        aliases = {len(operands): 0}
        operands.append(out)
        in_specs.append(whole)
    shape = parts[0][1].shape
    count = sum(raw.shape[0] for _, raw, *_ in parts)
    return pl.pallas_call(
        functools.partial(skew_kernel, which, [(part[0], part[3], part[5]) for part in parts]),
        in_specs=in_specs,
        out_specs=whole,
        out_shape=jax.ShapeDtypeStruct((1, energies) + shape[1:], jnp.float32),
        scratch_shapes=[pltpu.VMEM((count, len(which)) + shape[2:], jnp.float32), pltpu.SemaphoreType.DMA],
        input_output_aliases=aliases,
        compiler_params=pltpu.CompilerParams(vmem_limit_bytes=VMEM_LIMIT),
        name="skew",
    )(*operands)


def grid_moves(momenta, side):
    half = side // 2

    def number(momentum, row_half, row_low, col_half, col_low):
        return (momentum * side + row_half * half + row_low) * side + col_half * half + col_low

    over_columns, over_rows, near = ([], []), ([], []), []
    for momentum in range(momenta):
        for a in range(2):
            for row in range(half):
                for col in range(half):
                    b = 1 - a
                    here = number(momentum, a, row, b, col)
                    mirror = number(momentum, b, col, a, row)
                    by_columns = number(momentum, a, col, a, row)
                    by_rows = number(momentum, b, row, b, col)
                    over_columns[0].append((here, by_columns))
                    over_columns[1].append((by_rows, mirror))
                    over_rows[0].append((here, by_rows))
                    over_rows[1].append((by_columns, mirror))
                    if row != col:
                        near.append((number(momentum, a, row, a, col), number(momentum, a, col, a, row)))
    return over_columns, over_rows, near


def send(array, axes, pairs, what):
    with jax.named_scope(what):
        return lax.ppermute(array, axes, pairs)


def on_device(counts, near_cuts, green_lesser, screened, slot_table):
    momenta = lax.axis_size("ka")
    over_columns, over_rows, near_pairs = grid_moves(momenta, lax.axis_size("br"))
    groups = {}
    for stop, hop in enumerate(HOPS):
        groups.setdefault(hop % momenta, []).append(stop)
    spans = [(sum(counts[:run]), count) for run, count in enumerate(counts)]
    runs = len(spans)
    groups_near = list(zip((0, *near_cuts), (*near_cuts, runs)))

    tables = {}
    for shift in groups:
        table = slot_table
        if shift:
            table = lax.ppermute(table, "ka", [((k + shift) % momenta, k) for k in range(momenta)])
        tables[shift] = table.reshape(len(HOPS))
    green, inter = fetch(green_lesser, screened, BLOCKS)
    own_table, own_stops = tables.pop(0), groups.pop(0)

    terms = [{} for _ in spans]
    for some in (range(1), range(1, runs)):
        for shift, stops in groups.items():
            found = correlate(green, inter, tables[shift], stops, [spans[run] for run in some])
            for run, term in zip(some, found):
                terms[run][shift] = term

    def exchange(run):
        return [
            send(term, "ka", [(k, (k + shift) % momenta) for k in range(momenta)], f"momentum_{run}")
            for shift, term in terms[run].items()
        ]

    if runs > 1 and OWN_TIE:
        own_table, terms[0] = lax.optimization_barrier((own_table, terms[0]))
    own = correlate(green, inter, own_table, own_stops, spans)
    arrived = [exchange(run) for run in range(runs)]
    raws, by_columns, by_rows = [], [], []
    for run in range(runs):
        raw, over_first, over_second = mix(
            own[run],
            arrived[run],
            by_rows[run - 1] if run >= 1 else None,
            by_columns[run - 2] if run >= 2 else None,
        )
        raws.append(raw)
        by_columns.append(send(over_first, AXES, sum(over_columns, []), f"columns_{run}"))
        by_rows.append(send(over_second, AXES, sum(over_rows, []), f"rows_{run}"))
    nears, near_places = [], []
    for low, high in groups_near:
        some = raws[low:high]
        if NEAR_LAST and high == runs:
            some, _ = lax.optimization_barrier((some, by_rows[runs - 1]))
        near = send(pack(some), AXES, near_pairs, f"near_{low}")
        for run in range(low, high):
            nears.append(near)
            near_places.append(spans[run][0] - spans[low][0])
    by_columns.append(send(by_rows[-1], AXES, over_columns[1], f"columns_{runs}"))

    def part(run, fars, far_firsts):
        return spans[run][0], raws[run], nears[run], near_places[run], fars, far_firsts

    out = None
    for run in range(runs - 2):
        fars = [by_rows[run + 2], by_columns[run + 1]]
        if SKEW_TIE and run == 0:
            fars, _ = lax.optimization_barrier((fars, by_rows[runs - 1]))
        out = skew([part(run, fars, [0, 0])], (0, 1), NE, out)
    last = by_columns[runs - 1]
    if out is not None and TIE:
        last, out = lax.optimization_barrier((last, out))
    before = by_columns[runs - 2]
    if ROWS_LAST:
        before, _ = lax.optimization_barrier((before, by_rows[runs - 1]))
    by_rows.append(send(before, AXES, over_rows[1], f"rows_{runs}"))
    by_rows.append(send(last, AXES, over_rows[1], f"rows_{runs + 1}"))
    ends = (runs - 2, runs - 1)
    out = skew([part(run, [by_columns[run + 1]], [0]) for run in ends], (1,), NE, out)
    return skew([part(run, [by_rows[run + 2]], [0]) for run in ends], (0,), NE, out)


def solution(mesh):
    in_specs = (
        P("ka", None, None, "br", "bc"),
        P(None, None, None, "br", "bc"),
        P(None, "ka", None),
    )
    out_specs = P("ka", None, None, "br", "bc")
    return jax.shard_map(
        functools.partial(on_device, COUNTS, NEAR_CUTS), mesh=mesh, in_specs=in_specs, out_specs=out_specs, check_vma=False
    )
```

```python
import functools

import jax
import jax.numpy as jnp
from jax import lax
from jax.experimental import pallas as pl
from jax.experimental.pallas import tpu as pltpu
from jax.sharding import PartitionSpec as P

NE = 8
TIE = True
BLOCKS = 2
OWN_TIE = True
FLOPS = 20_000_000_000
COUNTS = (2,2,2,2)
NEAR_CUTS = (1,3)
HOPS = (0, 1, -1, 2, -2)
SUBLANES = 8
AXES = ("ka", "br", "bc")
VMEM_LIMIT = 32 * 1024 * 1024


def correlate_rows(green_ref, screened_ref, table_ref, stops, first, counts, out_refs, low, high):
    freqs = screened_ref.shape[1]
    energies = sum(counts)

    def rows_step(step, carry):
        at = pl.ds(pl.multiple_of(step * SUBLANES, SUBLANES), SUBLANES)

        def inter(freq, part):
            value = screened_ref[table_ref[stops[0]], freq, part, at, :]
            for stop in stops[1:]:
                value = value + screened_ref[table_ref[stop], freq, part, at, :]
            return value

        real = [None] * energies
        imag = [None] * energies
        weights = [(inter(freq, 0), inter(freq, 1)) for freq in range(freqs)]
        for lag in range(energies + freqs - 1):
            green_real = green_ref[0, first + lag, 0, at, :]
            green_imag = green_ref[0, first + lag, 1, at, :]
            for energy in range(energies):
                freq = energy + freqs - 1 - lag
                if 0 <= freq < freqs:
                    inter_real, inter_imag = weights[freq]
                    real_term = green_real * inter_imag + green_imag * inter_real
                    imag_term = green_real * inter_real - green_imag * inter_imag
                    if real[energy] is None:
                        real[energy], imag[energy] = -real_term, imag_term
                    else:
                        real[energy] = real[energy] - real_term
                        imag[energy] = imag[energy] + imag_term
        energy = 0
        for out_ref, count in zip(out_refs, counts):
            for place in range(count):
                out_ref[place, 0, at, :] = real[energy]
                out_ref[place, 1, at, :] = imag[energy]
                energy += 1
        return carry

    lax.fori_loop(low // SUBLANES, high // SUBLANES, rows_step, 0)


def fetch_kernel(blocks, green_hbm, screened_hbm, green_ref, screened_ref, sem):
    copies = []
    for which, (source, target) in enumerate(((screened_hbm, screened_ref), (green_hbm, green_ref))):
        rows = source.shape[3] // blocks
        for block in range(blocks):
            at = pl.ds(block * rows, rows)
            copies.append(
                pltpu.make_async_copy(source.at[:, :, :, at], target.at[:, :, :, at], sem.at[which, block])
            )
    for copy in copies:
        copy.start()
    for copy in copies:
        copy.wait()


def on_hbm(*arrays):
    return [pltpu.with_memory_space_constraint(array, pltpu.HBM) for array in arrays]


def fetch(green, screened, blocks):
    vmem = pl.BlockSpec(memory_space=pltpu.VMEM)
    return pl.pallas_call(
        functools.partial(fetch_kernel, blocks),
        in_specs=[pl.BlockSpec(memory_space=pltpu.HBM)] * 2,
        out_specs=[vmem] * 2,
        out_shape=[jax.ShapeDtypeStruct(array.shape, array.dtype) for array in (green, screened)],
        scratch_shapes=[pltpu.SemaphoreType.DMA((2, blocks))],
        compiler_params=pltpu.CompilerParams(vmem_limit_bytes=VMEM_LIMIT),
        name="fetch",
    )(*on_hbm(green, screened))


def run_shapes(green, spans):
    return [jax.ShapeDtypeStruct((count,) + green.shape[2:], jnp.float32) for _, count in spans]


def correlate_kernel(stops, first, counts, table_ref, green_ref, screened_ref, *out_refs):
    correlate_rows(
        green_ref, screened_ref, table_ref, stops, first, counts, out_refs, 0, green_ref.shape[3]
    )


def correlate(green, screened, table, stops, spans):
    if not spans:
        return []
    vmem = pl.BlockSpec(memory_space=pltpu.VMEM)
    counts = [count for _, count in spans]
    return pl.pallas_call(
        functools.partial(correlate_kernel, stops, spans[0][0], counts),
        in_specs=[pl.BlockSpec(memory_space=pltpu.SMEM), vmem, vmem],
        out_specs=[vmem] * len(spans),
        out_shape=run_shapes(green, spans),
        compiler_params=pltpu.CompilerParams(vmem_limit_bytes=VMEM_LIMIT),
        name="correlate",
    )(table, green, screened)


def place_of_device():
    row, col = lax.axis_index("br"), lax.axis_index("bc")
    half = lax.axis_size("br") // 2
    return (row // half) != (col // half), row == col


def mix_kernel(received, held, own_ref, *refs):
    recv_refs = refs[:received]
    held_refs = refs[received : received + sum(held)]
    raw_ref, col_ref, row_ref = refs[received + sum(held) :]
    far, _ = place_of_device()
    queue = list(held_refs)
    holds = [queue.pop(0) if has else None for has in held]
    count = own_ref.shape[0]
    for part, hold_ref, send_ref in zip((0, 1), holds, (col_ref, row_ref)):
        for place in range(send_ref.shape[0]):
            value = None
            if place < count:
                value = own_ref[place, part]
                for ref in recv_refs:
                    value = value + ref[place, part]
                raw_ref[place, part] = value
            if hold_ref is not None and place < hold_ref.shape[0]:
                kept = hold_ref[place]
                value = kept if value is None else jnp.where(far, value, kept)
            if value is not None:
                send_ref[place] = value


def mix(own, received, held_columns, held_rows):
    vmem = pl.BlockSpec(memory_space=pltpu.VMEM)
    held = [array is not None for array in (held_columns, held_rows)]
    holds = [array for array in (held_columns, held_rows) if array is not None]
    lengths = [max(own.shape[0], array.shape[0] if array is not None else 0) for array in (held_columns, held_rows)]
    shapes = [own.shape] + [(length,) + own.shape[2:] for length in lengths]
    return pl.pallas_call(
        functools.partial(mix_kernel, len(received), held),
        in_specs=[vmem] * (1 + len(received) + len(holds)),
        out_specs=[vmem] * 3,
        out_shape=[jax.ShapeDtypeStruct(shape, jnp.float32) for shape in shapes],
        compiler_params=pltpu.CompilerParams(vmem_limit_bytes=VMEM_LIMIT),
        name="mix", cost_estimate=pl.CostEstimate(flops=FLOPS, bytes_accessed=1000000, transcendentals=0),
    )(own, *received, *holds)


def pack_kernel(*refs):
    out_ref = refs[-1]
    far, _ = place_of_device()

    @pl.when(jnp.logical_not(far))
    def _():
        at = 0
        for ref in refs[:-1]:
            out_ref[pl.ds(at, ref.shape[0])] = ref[...]
            at += ref.shape[0]


def pack(raws):
    if len(raws) == 1:
        return raws[0]
    vmem = pl.BlockSpec(memory_space=pltpu.VMEM)
    return pl.pallas_call(
        pack_kernel,
        in_specs=[vmem] * len(raws),
        out_specs=vmem,
        out_shape=jax.ShapeDtypeStruct((sum(raw.shape[0] for raw in raws),) + raws[0].shape[1:], jnp.float32),
        compiler_params=pltpu.CompilerParams(vmem_limit_bytes=VMEM_LIMIT),
        name="pack",
    )(*raws)


def skew_kernel(which, places, *refs):
    width = 2 + len(which)
    parts = [refs[width * at : width * (at + 1)] for at in range(len(places))]
    out_ref, done_ref, sem = refs[-3:]
    far, own = place_of_device()
    start = places[0][0]

    def write(partner):
        for (raw_ref, near_ref, *far_refs), (first, near_first, far_firsts) in zip(parts, places):
            for at in range(raw_ref.shape[0]):
                for slot, (kind, far_ref, far_first) in enumerate(zip(which, far_refs, far_firsts)):
                    raw = raw_ref[at, kind]
                    mirror = partner(raw, near_ref, near_first + at, kind, far_ref, far_first + at).T
                    done_ref[first - start + at, slot] = (raw + mirror if kind else raw - mirror) * 0.5

    @pl.when(far)
    def _():
        write(lambda raw, near_ref, near_at, kind, far_ref, far_at: far_ref[far_at])

    @pl.when(jnp.logical_and(jnp.logical_not(far), jnp.logical_not(own)))
    def _():
        write(lambda raw, near_ref, near_at, kind, far_ref, far_at: near_ref[near_at, kind])

    @pl.when(own)
    def _():
        write(lambda raw, near_ref, near_at, kind, far_ref, far_at: raw)

    target = out_ref.at[0, pl.ds(start, done_ref.shape[0]), pl.ds(which[0], len(which))]
    copy = pltpu.make_async_copy(done_ref, target, sem)
    copy.start()
    copy.wait()


def skew(parts, which, energies, out):
    vmem = pl.BlockSpec(memory_space=pltpu.VMEM)
    whole = pl.BlockSpec(memory_space=pl.ANY)
    operands = [array for _, raw, near, _, fars, _ in parts for array in (raw, near, *fars)]
    in_specs = [vmem] * len(operands)
    aliases = {}
    if out is not None:
        aliases = {len(operands): 0}
        operands.append(out)
        in_specs.append(whole)
    shape = parts[0][1].shape
    count = sum(raw.shape[0] for _, raw, *_ in parts)
    return pl.pallas_call(
        functools.partial(skew_kernel, which, [(part[0], part[3], part[5]) for part in parts]),
        in_specs=in_specs,
        out_specs=whole,
        out_shape=jax.ShapeDtypeStruct((1, energies) + shape[1:], jnp.float32),
        scratch_shapes=[pltpu.VMEM((count, len(which)) + shape[2:], jnp.float32), pltpu.SemaphoreType.DMA],
        input_output_aliases=aliases,
        compiler_params=pltpu.CompilerParams(vmem_limit_bytes=VMEM_LIMIT),
        name="skew",
    )(*operands)


def grid_moves(momenta, side):
    half = side // 2

    def number(momentum, row_half, row_low, col_half, col_low):
        return (momentum * side + row_half * half + row_low) * side + col_half * half + col_low

    over_columns, over_rows, near = ([], []), ([], []), []
    for momentum in range(momenta):
        for a in range(2):
            for row in range(half):
                for col in range(half):
                    b = 1 - a
                    here = number(momentum, a, row, b, col)
                    mirror = number(momentum, b, col, a, row)
                    by_columns = number(momentum, a, col, a, row)
                    by_rows = number(momentum, b, row, b, col)
                    over_columns[0].append((here, by_columns))
                    over_columns[1].append((by_rows, mirror))
                    over_rows[0].append((here, by_rows))
                    over_rows[1].append((by_columns, mirror))
                    if row != col:
                        near.append((number(momentum, a, row, a, col), number(momentum, a, col, a, row)))
    return over_columns, over_rows, near


def send(array, axes, pairs, what):
    with jax.named_scope(what):
        return lax.ppermute(array, axes, pairs)


def on_device(counts, near_cuts, green_lesser, screened, slot_table):
    momenta = lax.axis_size("ka")
    over_columns, over_rows, near_pairs = grid_moves(momenta, lax.axis_size("br"))
    groups = {}
    for stop, hop in enumerate(HOPS):
        groups.setdefault(hop % momenta, []).append(stop)
    spans = [(sum(counts[:run]), count) for run, count in enumerate(counts)]
    runs = len(spans)
    groups_near = list(zip((0, *near_cuts), (*near_cuts, runs)))

    tables = {}
    for shift in groups:
        table = slot_table
        if shift:
            table = lax.ppermute(table, "ka", [((k + shift) % momenta, k) for k in range(momenta)])
        tables[shift] = table.reshape(len(HOPS))
    green, inter = fetch(green_lesser, screened, BLOCKS)
    own_table, own_stops = tables.pop(0), groups.pop(0)

    terms = [{} for _ in spans]
    for some in (range(1), range(1, runs)):
        for shift, stops in groups.items():
            found = correlate(green, inter, tables[shift], stops, [spans[run] for run in some])
            for run, term in zip(some, found):
                terms[run][shift] = term

    def exchange(run):
        return [
            send(term, "ka", [(k, (k + shift) % momenta) for k in range(momenta)], f"momentum_{run}")
            for shift, term in terms[run].items()
        ]

    if runs > 1 and OWN_TIE:
        own_table, terms[0] = lax.optimization_barrier((own_table, terms[0]))
    own = correlate(green, inter, own_table, own_stops, spans)
    arrived = [exchange(run) for run in range(runs)]
    raws, by_columns, by_rows = [], [], []
    for run in range(runs):
        raw, over_first, over_second = mix(
            own[run],
            arrived[run],
            by_rows[run - 1] if run >= 1 else None,
            by_columns[run - 2] if run >= 2 else None,
        )
        raws.append(raw)
        by_columns.append(send(over_first, AXES, sum(over_columns, []), f"columns_{run}"))
        by_rows.append(send(over_second, AXES, sum(over_rows, []), f"rows_{run}"))
    nears, near_places = [], []
    for low, high in groups_near:
        near = send(pack(raws[low:high]), AXES, near_pairs, f"near_{low}")
        for run in range(low, high):
            nears.append(near)
            near_places.append(spans[run][0] - spans[low][0])
    by_columns.append(send(by_rows[-1], AXES, over_columns[1], f"columns_{runs}"))

    def part(run, fars, far_firsts):
        return spans[run][0], raws[run], nears[run], near_places[run], fars, far_firsts

    out = None
    for run in range(runs - 2):
        out = skew([part(run, [by_rows[run + 2], by_columns[run + 1]], [0, 0])], (0, 1), NE, out)
    last = by_columns[runs - 1]
    if out is not None and TIE:
        last, out = lax.optimization_barrier((last, out))
    by_rows.append(send(by_columns[runs - 2], AXES, sum(over_rows, []), f"rows_{runs}"))
    by_rows.append(send(last, AXES, sum(over_rows, []), f"rows_{runs + 1}"))
    ends = (runs - 2, runs - 1)
    out = skew([part(run, [by_columns[run + 1]], [0]) for run in ends], (1,), NE, out)
    return skew([part(run, [by_rows[run + 2]], [0]) for run in ends], (0,), NE, out)


def solution(mesh):
    in_specs = (
        P("ka", None, None, "br", "bc"),
        P(None, None, None, "br", "bc"),
        P(None, "ka", None),
    )
    out_specs = P("ka", None, None, "br", "bc")
    return jax.shard_map(
        functools.partial(on_device, COUNTS, NEAR_CUTS), mesh=mesh, in_specs=in_specs, out_specs=out_specs, check_vma=False
    )
```
